256 devices in a mesh: row: 32 (over z, y_hi, core), col: 8 (over y_lo, x).
Axes of the slice: x: 4, y: 4 (y_hi: 2, y_lo: 2; y = y_hi * 2 + y_lo), z: 8, core: 2. Of those that a mesh axis runs over, the one named last changes fastest.
Arguments:
- img_emb: bfloat16 [131072, 1152], P(('row', 'col')), may hold values from -0.1796875 to 0.1796875
- txt_feat: bfloat16 [131072, 1152], P(('row', 'col')), may hold values from -6 to 6
- head_weight: bfloat16 [1152, 1152], replicated, may hold values from -0.1875 to 0.1875
- positive: int32 [256, 512], P(('row', 'col')), may hold values from 0 to 511, each once within a row
Outputs:
- img_grad: bfloat16 [131072, 1152], P(('row', 'col'))
- txt_grad: bfloat16 [131072, 1152], P(('row', 'col'))
- head_grad: float32 [1152, 1152], P('row', 'col')
The draws below stay inside these ranges and needn't reach their ends.
Inputs may be any that keep to these rules, and one draw needn't show every extreme that they name: Each row of positive is a permutation of the rows of one device.
All inputs are finite; a program needn't handle non-finite values.
Results may differ from the reference program's by a relative error of at most 0.015.
Values may be sent and summed in bfloat16 or wider, within the bound.
No kernel may reach another device: no remote copies, remote signals or barrier semaphores. Data moves between devices by JAX's collectives and lax.ppermute only.
A program may use at most 64 MiB of HBM per device.

```python
import jax
import jax.numpy as jnp
from jax import lax

E = 1152
ROWS = 512
TOTAL = 131072
N_ROW = 32
N_COL = 8


def level_of(rng, extent, pieces, least, high):
    loudness = 1.0
    for axis_at, blocks in pieces:
        steps = jax.random.uniform(jax.random.fold_in(jax.random.fold_in(rng, 6), axis_at), (blocks,), jnp.float32, least / len(pieces), high / len(pieces))
        loudness = loudness * jnp.repeat(jnp.exp(steps), extent[axis_at] // blocks).reshape((-1,) + (1,) * (len(extent) - 1 - axis_at))
    return loudness


def scatter_about(stream_key, dims, spread, reach, cuts=(), held_as=jnp.bfloat16):
    array = jax.random.normal(stream_key, dims, jnp.float32) * spread
    if len(cuts) > 0:
        array = level_of(stream_key, dims, cuts, -0.22, 0.18) * array
    return jnp.clip(array, min=-reach, max=reach).astype(held_as)


def setup_inputs(seed: int = 0) -> dict:
    arg_keys = jax.random.split(jax.random.key(seed), 5)
    return {
        "img_emb": scatter_about(arg_keys[0], (TOTAL, E), 0.03, 0.1796875, ((0, 256),)),
        "txt_feat": scatter_about(arg_keys[1], (TOTAL, E), 1.0, 6.0, ((0, 256),)),
        "head_weight": scatter_about(arg_keys[2], (E, E), E ** -0.5, 0.1875),
        "positive": jax.vmap(lambda own: jax.random.permutation(own, ROWS))(jax.random.split(arg_keys[3], (N_ROW * N_COL))).reshape((N_ROW * N_COL, ROWS)).astype(jnp.int32),
    }


scale_logit = 8.0
bias_logit = -2.0

def block_terms(zi, zt, labels):
    logits = scale_logit * lax.dot_general(zi, zt, (((1,), (1,)), ((), ())), preferred_element_type=jnp.float32) + bias_logit
    sign = jnp.where(labels, 1.0, -1.0).astype(jnp.float32)
    dsc = (-scale_logit * sign * jax.nn.sigmoid(-sign * logits)).astype(jnp.bfloat16)
    to_img = jnp.dot(dsc, zt, preferred_element_type=jnp.float32)
    to_txt = lax.dot_general(dsc, zi, (((0,), (0,)), ((), ())), preferred_element_type=jnp.float32)
    return (to_img, to_txt)

def reference(img_emb, txt_feat, head_weight, positive):
    devs = N_ROW * N_COL
    u = jnp.dot(txt_feat, head_weight, preferred_element_type=jnp.float32)
    tnorm = jnp.sqrt(lax.optimization_barrier(jnp.sum(u * u, axis=-1, keepdims=True)) + 1e-06)
    that = u / tnorm
    zt = that.astype(jnp.bfloat16)
    imgf = img_emb.astype(jnp.float32)
    inorm = jnp.sqrt(lax.optimization_barrier(jnp.sum(imgf * imgf, axis=-1, keepdims=True)) + 1e-06)
    ihat = imgf / inorm
    zi = ihat.astype(jnp.bfloat16)
    zt_blocks = zt.reshape(devs, ROWS, E)
    zi_blocks = zi.reshape(devs, ROWS, E)
    index = jnp.arange(devs, dtype=jnp.int32)
    first = jnp.bitwise_xor(index, N_ROW // 2 * N_COL)
    second = jnp.bitwise_xor(index, N_COL // 2)
    columns = jnp.arange(ROWS, dtype=jnp.int32)
    none = jnp.zeros((ROWS, ROWS), dtype=bool)

    def one(d):
        zi_d = zi_blocks[d]
        labels = positive[d][:, None] == columns[None, :]
        img_own, txt_own = block_terms(zi_d, zt_blocks[d], labels)
        img_one, txt_one = block_terms(zi_d, zt_blocks[first[d]], none)
        img_two, txt_two = block_terms(zi_d, zt_blocks[second[d]], none)
        dzi = img_own + img_one + img_two
        return (dzi, txt_own, txt_one.astype(jnp.bfloat16), txt_two.astype(jnp.bfloat16))
    dzi, txt_own, back_one, back_two = lax.map(one, index)
    dzt = txt_own + back_one[first].astype(jnp.float32) + back_two[second].astype(jnp.float32)
    dzi = dzi.reshape(devs * ROWS, E)
    dzt = dzt.reshape(devs * ROWS, E)
    img_grad = ((dzi - ihat * lax.optimization_barrier(jnp.sum(ihat * dzi, axis=-1, keepdims=True))) / inorm).astype(jnp.bfloat16)
    du = ((dzt - that * lax.optimization_barrier(jnp.sum(that * dzt, axis=-1, keepdims=True))) / tnorm).astype(jnp.bfloat16)
    txt_grad = lax.dot_general(du, head_weight, (((1,), (1,)), ((), ())), preferred_element_type=jnp.float32).astype(jnp.bfloat16)
    head_grad = lax.dot_general(txt_feat, du, (((0,), (0,)), ((), ())), preferred_element_type=jnp.float32) / devs
    return (img_grad, txt_grad, head_grad)
```

```python
import jax
import jax.numpy as jnp
from jax import lax
from jax.sharding import PartitionSpec as P

scale_logit = 8.0
bias_logit = -2.0
f32 = jnp.float32
bf16 = jnp.bfloat16


def from_partner(block, axis, mask):
    count = lax.axis_size(axis)
    return lax.ppermute(block, axis, [(low, low ^ mask) for low in range(count)])


def rows_by_rows(a, b):
    return lax.dot_general(a, b, (((1,), (1,)), ((), ())), preferred_element_type=f32)


def columns_by_columns(a, b):
    return lax.dot_general(a, b, (((0,), (0,)), ((), ())), preferred_element_type=f32)


def unit(img):
    wide = img.astype(f32)
    norm = jnp.sqrt(jnp.sum(wide * wide, axis=-1, keepdims=True) + 1e-06)
    hat = wide / norm
    return hat, norm, hat.astype(bf16)


def unpaired(zi, zt):
    logits = scale_logit * rows_by_rows(zi, zt) + bias_logit
    return (scale_logit * jax.nn.sigmoid(logits)).astype(bf16)


def paired(zi, zt, labels):
    logits = scale_logit * rows_by_rows(zi, zt) + bias_logit
    sign = jnp.where(labels, 1.0, -1.0).astype(f32)
    return (-scale_logit * sign * jax.nn.sigmoid(-sign * logits)).astype(bf16)


def shards(img_emb, txt_feat, head_weight, positive):
    rows, width = img_emb.shape
    n_row = lax.axis_size("row")
    n_col = lax.axis_size("col")
    row_mask = n_row // 2
    col_mask = n_col // 2
    share_rows = width // n_row
    share_cols = width // n_col
    half = rows // 2
    parts = [slice(0, half), slice(half, rows)]

    img_two = from_partner(img_emb, "col", col_mask)
    img_one = [from_partner(img_emb[p], "row", row_mask) for p in parts]

    u = jnp.dot(txt_feat, head_weight, preferred_element_type=f32)
    tnorm = jnp.sqrt(jnp.sum(u * u, axis=-1, keepdims=True) + 1e-06)
    that = u / tnorm
    zt = that.astype(bf16)
    txt_two = from_partner(zt, "col", col_mask)
    txt_one = [from_partner(zt[p], "row", row_mask) for p in parts]

    core = lax.axis_index("row") & 1
    lane = jnp.arange(width // 2, dtype=jnp.int32)
    place = lane // share_rows
    depth = n_row // 4
    block = (place % depth) * 4 + (place // depth) * 2
    source = block * share_rows + lane % share_rows
    column = jnp.arange(width, dtype=jnp.int32)[:, None]

    def pick(which):
        choose = (column == (source + which * share_rows)[None, :]).astype(bf16)
        return jnp.dot(txt_feat, choose, preferred_element_type=f32).astype(bf16)

    txt_mine = pick(core)
    txt_theirs = pick(1 - core)

    ihat, inorm, zi = unit(img_emb)
    columns = jnp.arange(rows, dtype=jnp.int32)
    labels = positive[0][:, None] == columns[None, :]
    dsc = paired(zi, zt, labels)
    dzi = jnp.dot(dsc, zt, preferred_element_type=f32)
    dzt = columns_by_columns(dsc, zi)

    for img in [img_two] + img_one:
        zi_from = unit(img)[2]
        dzt = dzt + columns_by_columns(unpaired(zi_from, zt), zi_from)

    du = ((dzt - that * jnp.sum(that * dzt, axis=-1, keepdims=True)) / tnorm).astype(bf16)
    head_theirs = columns_by_columns(du, txt_theirs).astype(bf16)
    head_theirs = from_partner(head_theirs, "row", 1)
    head = columns_by_columns(du, txt_mine) + head_theirs.astype(f32)
    head = lax.all_to_all(head.astype(bf16), "col", 0, 0, tiled=True)
    head = jnp.sum(head.reshape(n_col, share_cols, width // 2).astype(f32), axis=0).astype(bf16)
    head = head.reshape(share_cols, n_row // 2, share_rows).transpose(1, 0, 2)
    groups = [[z * 4 + y * 2 + c for y in range(2) for z in range(depth)] for c in range(2)]
    head = lax.all_to_all(head, "row", 0, 0, axis_index_groups=groups, tiled=True)
    head = jnp.sum(head.astype(f32), axis=0).T
    head_grad = head / (n_row * n_col)

    txt_grad = rows_by_rows(du, head_weight).astype(bf16)

    for zt_from in [txt_two] + txt_one:
        dzi = dzi + jnp.dot(unpaired(zi, zt_from), zt_from, preferred_element_type=f32)
    img_grad = ((dzi - ihat * jnp.sum(ihat * dzi, axis=-1, keepdims=True)) / inorm).astype(bf16)
    return (img_grad, txt_grad, head_grad)


def solution(mesh):
    return jax.shard_map(
        shards,
        mesh=mesh,
        in_specs=(P(("row", "col"), None), P(("row", "col"), None), P(), P(("row", "col"), None)),
        out_specs=(P(("row", "col"), None), P(("row", "col"), None), P("row", "col")),
        check_vma=False,
    )
```

```python
import functools

import jax
import jax.numpy as jnp
from jax import lax
from jax.experimental import pallas as pl
from jax.experimental.pallas import tpu as pltpu
from jax.sharding import PartitionSpec as P

scale_logit = 8.0
bias_logit = -2.0
f32 = jnp.float32
bf16 = jnp.bfloat16
MIB = 1 << 20
X_ONE = 6e9
X_END = 3e9


def from_partner(block, axis, mask):
    count = lax.axis_size(axis)
    return lax.ppermute(block, axis, [(low, low ^ mask) for low in range(count)])


def nt(a, b):
    return lax.dot_general(a, b, (((1,), (1,)), ((), ())), preferred_element_type=f32)


def tn(a, b):
    return lax.dot_general(a, b, (((0,), (0,)), ((), ())), preferred_element_type=f32)


def nn(a, b):
    return jnp.dot(a, b, preferred_element_type=f32)


def unit(block):
    wide = block.astype(f32)
    norm = jnp.sqrt(jnp.sum(wide * wide, axis=-1, keepdims=True) + 1e-06)
    return wide / norm, norm


def unpaired(products):
    return (scale_logit / (1.0 + jnp.exp(-bias_logit - scale_logit * products))).astype(bf16)


def paired(products, labels):
    logits = scale_logit * products + bias_logit
    size = scale_logit / (1.0 + jnp.exp(jnp.where(labels, logits, -logits)))
    return jnp.where(labels, -size, size).astype(bf16)


def tiles(rows, size):
    return [slice(at, at + size) for at in range(0, rows, size)]


def text_kernel(txt_ref, head_ref, mine_ref, theirs_ref, that_ref, tnorm_ref, zt_ref, low_ref, high_ref, my_ref, their_ref, choose):
    width = head_ref.shape[0]

    @pl.when(pl.program_id(0) == 0)
    def _():
        for k, source_ref in enumerate((mine_ref, theirs_ref)):
            index = lax.broadcasted_iota(jnp.int32, (width, source_ref.shape[1]), 0)
            choose[k] = jnp.where(source_ref[...] == index, 1.0, 0.0).astype(bf16)

    txt = txt_ref[...]
    u = nn(txt, head_ref[...])
    tnorm = jnp.sqrt(jnp.sum(u * u, axis=-1, keepdims=True) + 1e-06)
    that = u / tnorm
    that_ref[...] = that
    tnorm_ref[...] = tnorm
    zt_ref[...] = that.astype(bf16)

    @pl.when(pl.program_id(0) == 0)
    def _():
        low_ref[...] = that.astype(bf16)

    @pl.when(pl.program_id(0) == 1)
    def _():
        high_ref[...] = that.astype(bf16)

    my_ref[...] = nn(txt, choose[0]).astype(bf16)
    their_ref[...] = nn(txt, choose[1]).astype(bf16)


def load_units(pieces, zi):
    at = 0
    for piece in pieces:
        zi[at : at + piece.shape[0], :] = unit(piece[...])[0].astype(bf16)
        at += piece.shape[0]


def text_main_kernel(tile, img_ref, two_ref, one_ref, zt_ref, across_ref, zi_ref, dzt_ref, zi):
    load_units([img_ref], zi_ref)
    load_units([two_ref, one_ref], zi)
    for t in tiles(zt_ref.shape[0], tile):
        zt = zt_ref[t, :]
        products = nt(zt, zi_ref[...])
        index = lax.broadcasted_iota(jnp.int32, products.shape, 0) + t.start
        total = nn(paired(products, across_ref[...] == index), zi_ref[...])
        dzt_ref[t, :] = total + nn(unpaired(nt(zt, zi[...])), zi[...])


def text_end_kernel(tile, count, *refs):
    pieces = refs[:count]
    zt_ref, dzt_ref, that_ref, tnorm_ref, txt_ref, du_ref, head_ref, zi = refs[count:]
    load_units(pieces, zi)
    for t in tiles(zt_ref.shape[0], tile):
        dsc = unpaired(nt(zt_ref[t, :], zi[...]))
        dzt = dzt_ref[t, :] + nn(dsc, zi[...])
        that = that_ref[t, :]
        along = jnp.sum(that * dzt, axis=-1, keepdims=True)
        du_ref[t, :] = ((dzt - that * along) / tnorm_ref[t, :]).astype(bf16)
    for t in tiles(du_ref.shape[1], 384):
        head_ref[t, :] = tn(du_ref[:, t], txt_ref[...]).astype(bf16)


def head_kernel(du_ref, txt_ref, got_ref, out_ref):
    for t in tiles(du_ref.shape[1], 384):
        mine = tn(du_ref[:, t], txt_ref[...])
        out_ref[t, :] = (mine + got_ref[t, :].astype(f32)).astype(bf16)


def txt_grad_kernel(tile, du_ref, head_ref, out_ref):
    for t in tiles(du_ref.shape[0], tile):
        out_ref[t, :] = nt(du_ref[t, :], head_ref[...]).astype(bf16)


def gather_kernel(pad, fold, got_ref, out_ref):
    total = got_ref[0].astype(f32)
    for k in range(1, got_ref.shape[0]):
        total = total + got_ref[k].astype(f32)
    high = total.shape[0] // fold
    for i in range(out_ref.shape[0]):
        cut = [total[high * k : high * (k + 1), pad * i : pad * (i + 1)] for k in range(fold)]
        rest = out_ref.shape[2] - fold * pad
        cut.append(jnp.zeros((high, rest), f32))
        out_ref[i] = jnp.concatenate(cut, axis=1).astype(bf16)


def finish_kernel(pad, fold, devices, got_ref, out_ref):
    total = got_ref[0].astype(f32)
    for k in range(1, got_ref.shape[0]):
        total = total + got_ref[k].astype(f32)
    turned = (total * (1.0 / devices)).T
    rows = out_ref.shape[0]
    cut = [turned[pad * k : pad * k + rows] for k in range(fold)]
    out_ref[...] = jnp.concatenate(cut, axis=1)


def image_main_kernel(tile, zi_ref, zt_ref, low_ref, high_ref, down_ref, dzi_ref, two_ref):
    two_ref[: low_ref.shape[0], :] = low_ref[...]
    two_ref[low_ref.shape[0] :, :] = high_ref[...]
    for t in tiles(zi_ref.shape[0], tile):
        zi = zi_ref[t, :]
        products = nt(zi, zt_ref[...])
        index = lax.broadcasted_iota(jnp.int32, products.shape, 1)
        total = nn(paired(products, down_ref[t, :] == index), zt_ref[...])
        dzi_ref[t, :] = total + nn(unpaired(nt(zi, two_ref[...])), two_ref[...])


def image_side_kernel(tile, one_ref, zi_ref, dzi_ref, out_ref):
    for t in tiles(zi_ref.shape[0], tile):
        dsc = unpaired(nt(zi_ref[t, :], one_ref[...]))
        out_ref[t, :] = dzi_ref[t, :] + nn(dsc, one_ref[...])


def image_end_kernel(tile, one_ref, zi_ref, dzi_ref, img_ref, out_ref):
    for t in tiles(zi_ref.shape[0], tile):
        dsc = unpaired(nt(zi_ref[t, :], one_ref[...]))
        dzi = dzi_ref[t, :] + nn(dsc, one_ref[...])
        ihat, inorm = unit(img_ref[t, :])
        along = jnp.sum(ihat * dzi, axis=-1, keepdims=True)
        out_ref[t, :] = ((dzi - ihat * along) / inorm).astype(bf16)


def call(kernel, outs, args, scratch=(), aliases=None, name=None, flops=1):
    return pl.pallas_call(
        kernel,
        out_shape=outs,
        scratch_shapes=list(scratch),
        input_output_aliases=aliases or {},
        compiler_params=pltpu.CompilerParams(vmem_limit_bytes=12 * MIB),
        cost_estimate=pl.CostEstimate(flops=flops, bytes_accessed=1, transcendentals=0),
        name=name,
    )(*args)


def shards(img_emb, txt_feat, head_weight, positive):
    rows, width = img_emb.shape
    n_row = lax.axis_size("row")
    n_col = lax.axis_size("col")
    share_rows = width // n_row
    share_cols = width // n_col
    depth = n_row // 4
    tile = min(128, rows)
    shape = jax.ShapeDtypeStruct

    def after(value, *others):
        return lax.optimization_barrier((value,) + others)[0]

    half = rows // 2
    img_a, img_b = img_emb[:half], img_emb[half:]
    txt_feat = after(txt_feat, img_a, img_b)
    img_two = from_partner(after(img_emb, img_a, img_b), "col", n_col // 2)
    img_a = from_partner(img_a, "row", n_row // 2)
    img_b = from_partner(img_b, "row", n_row // 2)

    core = lax.axis_index("row") & 1
    pad = -(-share_rows // 8) * 8
    lanes = 2 * depth * pad
    lane = jnp.arange(lanes, dtype=jnp.int32)
    place = lane // pad
    inner = lane % pad
    block = (place % depth) * 4 + (place // depth) * 2

    def sources(which):
        return jnp.where(inner < share_rows, (block + which) * share_rows + inner, -1)[None, :]

    step = rows // 2
    that, tnorm, zt, zt_low, zt_high, txt_mine, txt_theirs = pl.pallas_call(
        text_kernel,
        grid=(2,),
        in_specs=[
            pl.BlockSpec((step, width), lambda i: (i, 0)),
            pl.BlockSpec((width, width), lambda i: (0, 0)),
            pl.BlockSpec((1, lanes), lambda i: (0, 0)),
            pl.BlockSpec((1, lanes), lambda i: (0, 0)),
        ],
        out_specs=[
            pl.BlockSpec((step, width), lambda i: (i, 0)),
            pl.BlockSpec((step, 1), lambda i: (i, 0)),
            pl.BlockSpec((step, width), lambda i: (i, 0)),
            pl.BlockSpec((step, width), lambda i: (0, 0)),
            pl.BlockSpec((step, width), lambda i: (0, 0)),
            pl.BlockSpec((step, lanes), lambda i: (i, 0)),
            pl.BlockSpec((step, lanes), lambda i: (i, 0)),
        ],
        out_shape=[
            shape((rows, width), f32),
            shape((rows, 1), f32),
            shape((rows, width), bf16),
            shape((step, width), bf16),
            shape((step, width), bf16),
            shape((rows, lanes), bf16),
            shape((rows, lanes), bf16),
        ],
        scratch_shapes=[pltpu.VMEM((2, width, lanes), bf16)],
        compiler_params=pltpu.CompilerParams(vmem_limit_bytes=16 * MIB),
        cost_estimate=pl.CostEstimate(flops=1, bytes_accessed=1, transcendentals=0),
        name="text",
    )(txt_feat, head_weight, sources(core), sources(1 - core))
    txt_two = [from_partner(part, "col", n_col // 2) for part in (zt_low, zt_high)]

    wide = shape((rows, width), f32)
    narrow = shape((rows, width), bf16)
    zi, dzt = call(
        functools.partial(text_main_kernel, tile),
        [narrow, wide],
        [img_emb, img_two, img_a, zt, positive],
        [pltpu.VMEM((rows + half, width), bf16)],
        name="text_main",
    )
    du, head = call(
        functools.partial(text_end_kernel, tile, 1),
        [narrow, shape((width, lanes), bf16)],
        [img_b, zt, dzt, that, tnorm, txt_theirs],
        [pltpu.VMEM((half, width), bf16)],
        name="text_end",
    )
    head = from_partner(after(head, *txt_two), "row", 1)
    head = call(
        head_kernel,
        shape((width, lanes), bf16),
        [du, txt_mine, head],
        name="head",
    )
    txt_a = from_partner(after(zt_low, du), "row", n_row // 2)
    du_late = after(du, head)
    head = lax.all_to_all(head.reshape(n_col, share_cols, lanes), "col", 0, 0, tiled=True)
    txt_grad = call(
        functools.partial(txt_grad_kernel, tile), narrow, [du_late, head_weight], name="txt_grad"
    )
    dzi = call(
        functools.partial(image_main_kernel, tile),
        wide,
        [zi, zt, *txt_two, after(positive, txt_grad).reshape(rows, 1)],
        [pltpu.VMEM((rows, width), bf16)],
        name="image_main",
    )
    dzi = call(
        functools.partial(image_side_kernel, tile),
        wide,
        [txt_a, zi, dzi],
        (),
        {2: 0},
        name="image_one",
        flops=int(X_ONE),
    )
    head = after(head, dzi)
    txt_b = from_partner(after(zt_high, dzi), "row", n_row // 2)
    fold = 3
    head = call(
        functools.partial(gather_kernel, pad, fold),
        shape((2 * depth, share_cols // fold, 128), bf16),
        [head],
        name="gather",
    )
    groups = [[z * 4 + y * 2 + c for y in range(2) for z in range(depth)] for c in range(2)]
    head = lax.all_to_all(head, "row", 0, 0, axis_index_groups=groups, tiled=True)
    img_grad = call(
        functools.partial(image_end_kernel, tile),
        narrow,
        [txt_b, zi, dzi, img_emb],
        name="image_end",
        flops=int(X_END),
    )
    head_grad = call(
        functools.partial(finish_kernel, pad, fold, n_row * n_col),
        shape((share_rows, share_cols), f32),
        [after(head, img_grad)],
        name="finish",
    )
    return (img_grad, txt_grad, head_grad)


def solution(mesh):
    return jax.shard_map(
        shards,
        mesh=mesh,
        in_specs=(P(("row", "col"), None), P(("row", "col"), None), P(), P(("row", "col"), None)),
        out_specs=(P(("row", "col"), None), P(("row", "col"), None), P("row", "col")),
        check_vma=False,
    )
```

```python
import functools

import jax
import jax.numpy as jnp
from jax import lax
from jax.experimental import pallas as pl
from jax.experimental.pallas import tpu as pltpu
from jax.sharding import PartitionSpec as P

scale_logit = 8.0
bias_logit = -2.0
f32 = jnp.float32
bf16 = jnp.bfloat16
MIB = 1 << 20
X_FIRST = 6e9
X_END = 3e9


def from_partner(block, axis, mask):
    count = lax.axis_size(axis)
    return lax.ppermute(block, axis, [(low, low ^ mask) for low in range(count)])


def turn(block, by):
    count = lax.axis_size("row")
    return lax.ppermute(block, "row", [(at, (at + 4 * by) % count) for at in range(count)])


def nt(a, b):
    return lax.dot_general(a, b, (((1,), (1,)), ((), ())), preferred_element_type=f32)


def tn(a, b):
    return lax.dot_general(a, b, (((0,), (0,)), ((), ())), preferred_element_type=f32)


def nn(a, b):
    return jnp.dot(a, b, preferred_element_type=f32)


def unit(block):
    wide = block.astype(f32)
    back = 1.0 / jnp.sqrt(jnp.sum(wide * wide, axis=-1, keepdims=True) + 1e-06)
    return wide * back, back


def unpaired(products):
    return (scale_logit / (1.0 + jnp.exp(-bias_logit - scale_logit * products))).astype(bf16)


def paired(products, labels):
    logits = scale_logit * products + bias_logit
    size = scale_logit / (1.0 + jnp.exp(jnp.where(labels, logits, -logits)))
    return jnp.where(labels, -size, size).astype(bf16)


def tiles(rows, size):
    return [slice(at, at + size) for at in range(0, rows, size)]


def text_kernel(txt_ref, head_ref, mine_ref, theirs_ref, that_ref, back_ref, zt_ref, low_ref, high_ref, my_ref, their_ref, choose):
    width = head_ref.shape[0]

    @pl.when(pl.program_id(0) == 0)
    def _():
        for k, source_ref in enumerate((mine_ref, theirs_ref)):
            index = lax.broadcasted_iota(jnp.int32, (width, source_ref.shape[1]), 0)
            choose[k] = jnp.where(source_ref[...] == index, 1.0, 0.0).astype(bf16)

    txt = txt_ref[...]
    u = nn(txt, head_ref[...])
    back = 1.0 / jnp.sqrt(jnp.sum(u * u, axis=-1, keepdims=True) + 1e-06)
    that = u * back
    that_ref[...] = that
    back_ref[...] = back
    zt_ref[...] = that.astype(bf16)

    @pl.when(pl.program_id(0) == 0)
    def _():
        low_ref[...] = that.astype(bf16)

    @pl.when(pl.program_id(0) == 1)
    def _():
        high_ref[...] = that.astype(bf16)

    my_ref[...] = nn(txt, choose[0]).astype(bf16)
    their_ref[...] = nn(txt, choose[1]).astype(bf16)


def load_units(pieces, zi):
    at = 0
    for piece in pieces:
        zi[at : at + piece.shape[0], :] = unit(piece[...])[0].astype(bf16)
        at += piece.shape[0]


def text_main_kernel(tile, img_ref, two_ref, zt_ref, across_ref, zi_ref, dzt_ref, zi):
    load_units([img_ref], zi_ref)
    load_units([two_ref], zi)
    for t in tiles(zt_ref.shape[0], tile):
        zt = zt_ref[t, :]
        products = nt(zt, zi_ref[...])
        index = lax.broadcasted_iota(jnp.int32, products.shape, 0) + t.start
        total = nn(paired(products, across_ref[...] == index), zi_ref[...])
        dzt_ref[t, :] = total + nn(unpaired(nt(zt, zi[...])), zi[...])


def text_end_kernel(tile, count, *refs):
    pieces = refs[:count]
    zt_ref, dzt_ref, that_ref, back_ref, txt_ref, du_ref, head_ref, zi = refs[count:]
    load_units(pieces, zi)
    for t in tiles(zt_ref.shape[0], tile):
        dsc = unpaired(nt(zt_ref[t, :], zi[...]))
        dzt = dzt_ref[t, :] + nn(dsc, zi[...])
        that = that_ref[t, :]
        along = jnp.sum(that * dzt, axis=-1, keepdims=True)
        du_ref[t, :] = ((dzt - that * along) * back_ref[t, :]).astype(bf16)
    for t in tiles(du_ref.shape[1], 384):
        head_ref[t, :] = tn(du_ref[:, t], txt_ref[...]).astype(bf16)


def head_kernel(du_ref, txt_ref, got_ref, out_ref):
    for t in tiles(du_ref.shape[1], 384):
        mine = tn(du_ref[:, t], txt_ref[...])
        out_ref[t, :] = (mine + got_ref[t, :].astype(f32)).astype(bf16)


def txt_grad_kernel(tile, du_ref, head_ref, out_ref):
    for t in tiles(du_ref.shape[0], tile):
        out_ref[t, :] = nt(du_ref[t, :], head_ref[...]).astype(bf16)


def gather_kernel(pad, fold, got_ref, out_ref):
    total = got_ref[0].astype(f32)
    for k in range(1, got_ref.shape[0]):
        total = total + got_ref[k].astype(f32)
    high = total.shape[0] // fold
    for i in range(out_ref.shape[0]):
        cut = [total[high * k : high * (k + 1), pad * i : pad * (i + 1)] for k in range(fold)]
        rest = out_ref.shape[2] - fold * pad
        cut.append(jnp.zeros((high, rest), f32))
        out_ref[i] = jnp.concatenate(cut, axis=1).astype(bf16)


def image_main_kernel(tile, zi_ref, zt_ref, low_ref, high_ref, down_ref, dzi_ref, two_ref):
    two_ref[: low_ref.shape[0], :] = low_ref[...]
    two_ref[low_ref.shape[0] :, :] = high_ref[...]
    for t in tiles(zi_ref.shape[0], tile):
        zi = zi_ref[t, :]
        products = nt(zi, zt_ref[...])
        index = lax.broadcasted_iota(jnp.int32, products.shape, 1)
        total = nn(paired(products, down_ref[t, :] == index), zt_ref[...])
        dzi_ref[t, :] = total + nn(unpaired(nt(zi, two_ref[...])), two_ref[...])


def column_kernel(across_ref, out_ref):
    wide = jnp.broadcast_to(across_ref[...].astype(f32), (128, across_ref.shape[1]))
    out_ref[...] = wide.T[:, :1].astype(jnp.int32)


def image_end_kernel(tile, low_ref, high_ref, zi_ref, dzi_ref, img_ref, out_ref, zt):
    zt[: low_ref.shape[0], :] = low_ref[...]
    zt[low_ref.shape[0] :, :] = high_ref[...]
    for t in tiles(zi_ref.shape[0], tile):
        dsc = unpaired(nt(zi_ref[t, :], zt[...]))
        dzi = dzi_ref[t, :] + nn(dsc, zt[...])
        ihat, back = unit(img_ref[t, :])
        along = jnp.sum(ihat * dzi, axis=-1, keepdims=True)
        out_ref[t, :] = ((dzi - ihat * along) * back).astype(bf16)


def finish_kernel(pad, fold, devices, got_ref, out_ref):
    total = got_ref[0].astype(f32)
    for k in range(1, got_ref.shape[0]):
        total = total + got_ref[k].astype(f32)
    turned = (total * (1.0 / devices)).T
    rows = out_ref.shape[0]
    out_ref[...] = jnp.concatenate([turned[pad * k : pad * k + rows] for k in range(fold)], axis=1)


def call(kernel, outs, args, scratch=(), aliases=None, name=None, flops=1):
    return pl.pallas_call(
        kernel,
        out_shape=outs,
        scratch_shapes=list(scratch),
        input_output_aliases=aliases or {},
        compiler_params=pltpu.CompilerParams(vmem_limit_bytes=20 * MIB),
        cost_estimate=pl.CostEstimate(flops=flops, bytes_accessed=1, transcendentals=0),
        name=name,
    )(*args)


def shards(img_emb, txt_feat, head_weight, positive):
    rows, width = img_emb.shape
    n_row = lax.axis_size("row")
    n_col = lax.axis_size("col")
    share_rows = width // n_row
    share_cols = width // n_col
    depth = n_row // 4
    tile = rows
    shape = jax.ShapeDtypeStruct

    def after(value, *others):
        return lax.optimization_barrier((value,) + others)[0]

    half = rows // 2
    img_one = from_partner(img_emb, "row", n_row // 2)
    img_two = from_partner(img_emb, "col", n_col // 2)

    core = lax.axis_index("row") & 1
    pad = -(-share_rows // 8) * 8
    lanes = 2 * depth * pad
    lane = jnp.arange(lanes, dtype=jnp.int32)
    place = lane // pad
    inner = lane % pad
    block = (place % depth) * 4 + (place // depth) * 2

    def sources(which):
        return jnp.where(inner < share_rows, (block + which) * share_rows + inner, -1)[None, :]

    step = rows // 2
    that, tback, zt, zt_low, zt_high, txt_mine, txt_theirs = pl.pallas_call(
        text_kernel,
        grid=(2,),
        in_specs=[
            pl.BlockSpec((step, width), lambda i: (i, 0)),
            pl.BlockSpec((width, width), lambda i: (0, 0)),
            pl.BlockSpec((1, lanes), lambda i: (0, 0)),
            pl.BlockSpec((1, lanes), lambda i: (0, 0)),
        ],
        out_specs=[
            pl.BlockSpec((step, width), lambda i: (i, 0)),
            pl.BlockSpec((step, 1), lambda i: (i, 0)),
            pl.BlockSpec((step, width), lambda i: (i, 0)),
            pl.BlockSpec((step, width), lambda i: (0, 0)),
            pl.BlockSpec((step, width), lambda i: (0, 0)),
            pl.BlockSpec((step, lanes), lambda i: (i, 0)),
            pl.BlockSpec((step, lanes), lambda i: (i, 0)),
        ],
        out_shape=[
            shape((rows, width), f32),
            shape((rows, 1), f32),
            shape((rows, width), bf16),
            shape((step, width), bf16),
            shape((step, width), bf16),
            shape((rows, lanes), bf16),
            shape((rows, lanes), bf16),
        ],
        scratch_shapes=[pltpu.VMEM((2, width, lanes), bf16)],
        compiler_params=pltpu.CompilerParams(vmem_limit_bytes=16 * MIB),
        cost_estimate=pl.CostEstimate(flops=1, bytes_accessed=1, transcendentals=0),
        name="text",
    )(txt_feat, head_weight, sources(core), sources(1 - core))
    txt_two = [from_partner(part, "col", n_col // 2) for part in (zt_low, zt_high)]

    wide = shape((rows, width), f32)
    narrow = shape((rows, width), bf16)
    zi, dzt = call(
        functools.partial(text_main_kernel, tile),
        [narrow, wide],
        [img_emb, img_two, zt, positive],
        [pltpu.VMEM((rows, width), bf16)],
        name="text_main",
    )
    du, head = call(
        functools.partial(text_end_kernel, tile, 1),
        [narrow, shape((width, lanes), bf16)],
        [img_one, zt, after(dzt, *txt_two), that, tback, txt_theirs],
        [pltpu.VMEM((rows, width), bf16)],
        name="text_end",
    )
    head = from_partner(head, "row", 1)
    head = call(
        head_kernel,
        shape((width, lanes), bf16),
        [du, txt_mine, head],
        name="head",
    )
    hop = depth // 4
    txt_a = turn(after(zt_low, du), hop)
    txt_b = turn(after(zt_high, du), -hop)
    du_late = after(du, head)
    head = lax.all_to_all(head.reshape(n_col, share_cols, lanes), "col", 0, 0, tiled=True)
    txt_grad = call(
        functools.partial(txt_grad_kernel, tile), narrow, [du_late, head_weight], name="txt_grad"
    )
    down = call(
        column_kernel,
        shape((rows, 1), jnp.int32),
        [after(positive, txt_a, txt_b, txt_grad)],
        name="column",
        flops=int(X_FIRST),
    )
    txt_a = turn(after(txt_a, down), hop)
    txt_b = turn(after(txt_b, down), -hop)
    head = after(head, down, txt_grad)
    fold = 3
    head = call(
        functools.partial(gather_kernel, pad, fold),
        shape((2 * depth, share_cols // fold, 128), bf16),
        [head],
        name="gather",
    )
    dzi = call(
        functools.partial(image_main_kernel, tile),
        wide,
        [zi, zt, *txt_two, after(down, head)],
        [pltpu.VMEM((rows, width), bf16)],
        name="image_main",
    )
    groups = [[z * 4 + y * 2 + c for y in range(2) for z in range(depth)] for c in range(2)]
    head = lax.all_to_all(head, "row", 0, 0, axis_index_groups=groups, tiled=True)
    img_grad = call(
        functools.partial(image_end_kernel, tile),
        narrow,
        [txt_a, txt_b, zi, dzi, img_emb],
        [pltpu.VMEM((rows, width), bf16)],
        name="image_end",
        flops=int(X_END),
    )
    head_grad = call(
        functools.partial(finish_kernel, pad, fold, n_row * n_col),
        shape((share_rows, share_cols), f32),
        [after(head, img_grad)],
        name="finish",
    )
    return (img_grad, txt_grad, head_grad)


def solution(mesh):
    return jax.shard_map(
        shards,
        mesh=mesh,
        in_specs=(P(("row", "col"), None), P(("row", "col"), None), P(), P(("row", "col"), None)),
        out_specs=(P(("row", "col"), None), P(("row", "col"), None), P("row", "col")),
        check_vma=False,
    )
```

```python
import functools

import jax
import jax.numpy as jnp
from jax import lax
from jax.experimental import pallas as pl
from jax.experimental.pallas import tpu as pltpu
from jax.sharding import PartitionSpec as P

scale_logit = 8.0
bias_logit = -2.0
f32 = jnp.float32
bf16 = jnp.bfloat16
MIB = 1 << 20
X_FIRST = 6.5e9
X_FINISH = 6e9
X_END = 3e9


def from_partner(block, axis, mask):
    count = lax.axis_size(axis)
    return lax.ppermute(block, axis, [(low, low ^ mask) for low in range(count)])


def turn(block, by):
    count = lax.axis_size("row")
    return lax.ppermute(block, "row", [(at, (at + 4 * by) % count) for at in range(count)])


def nt(a, b):
    return lax.dot_general(a, b, (((1,), (1,)), ((), ())), preferred_element_type=f32)


def tn(a, b):
    return lax.dot_general(a, b, (((0,), (0,)), ((), ())), preferred_element_type=f32)


def nn(a, b):
    return jnp.dot(a, b, preferred_element_type=f32)


def unit(block):
    wide = block.astype(f32)
    back = 1.0 / jnp.sqrt(jnp.sum(wide * wide, axis=-1, keepdims=True) + 1e-06)
    return wide * back, back


def unpaired(products):
    return (scale_logit / (1.0 + jnp.exp(-bias_logit - scale_logit * products))).astype(bf16)


def paired(products, labels):
    logits = scale_logit * products + bias_logit
    size = scale_logit / (1.0 + jnp.exp(jnp.where(labels, logits, -logits)))
    return jnp.where(labels, -size, size).astype(bf16)


def tiles(rows, size):
    return [slice(at, at + size) for at in range(0, rows, size)]


def text_kernel(txt_ref, head_ref, mine_ref, theirs_ref, that_ref, back_ref, zt_ref, low_ref, high_ref, my_ref, their_ref, choose):
    width = head_ref.shape[0]

    @pl.when(pl.program_id(0) == 0)
    def _():
        for k, source_ref in enumerate((mine_ref, theirs_ref)):
            index = lax.broadcasted_iota(jnp.int32, (width, source_ref.shape[1]), 0)
            choose[k] = jnp.where(source_ref[...] == index, 1.0, 0.0).astype(bf16)

    txt = txt_ref[...]
    u = nn(txt, head_ref[...])
    back = 1.0 / jnp.sqrt(jnp.sum(u * u, axis=-1, keepdims=True) + 1e-06)
    that = u * back
    that_ref[...] = that
    back_ref[...] = back
    zt_ref[...] = that.astype(bf16)

    @pl.when(pl.program_id(0) == 0)
    def _():
        low_ref[...] = that.astype(bf16)

    @pl.when(pl.program_id(0) == 1)
    def _():
        high_ref[...] = that.astype(bf16)

    my_ref[...] = nn(txt, choose[0]).astype(bf16)
    their_ref[...] = nn(txt, choose[1]).astype(bf16)


def load_units(pieces, zi):
    at = 0
    for piece in pieces:
        for c in tiles(piece.shape[0], 32):
            zi[at + c.start : at + c.stop, :] = unit(piece[c, :])[0].astype(bf16)
        at += piece.shape[0]


def text_main_kernel(tile, img_ref, two_ref, zt_ref, across_ref, zi_ref, dzt_ref, zi):
    load_units([img_ref], zi_ref)
    load_units([two_ref], zi)
    for t in tiles(zt_ref.shape[0], tile):
        zt = zt_ref[t, :]
        products = nt(zt, zi_ref[...])
        index = lax.broadcasted_iota(jnp.int32, products.shape, 0) + t.start
        total = nn(paired(products, across_ref[...] == index), zi_ref[...])
        dzt_ref[t, :] = total + nn(unpaired(nt(zt, zi[...])), zi[...])


def text_end_kernel(tile, count, *refs):
    pieces = refs[:count]
    zt_ref, dzt_ref, that_ref, back_ref, txt_ref, du_ref, head_ref, zi, last = refs[count:]
    load_units(pieces, zi)
    for t in tiles(zt_ref.shape[0], tile):
        dsc = unpaired(nt(zt_ref[t, :], zi[...]))
        last[t, :] = nn(dsc, zi[...])
    for c in tiles(zt_ref.shape[0], 32):
        dzt = dzt_ref[c, :] + last[c, :]
        that = that_ref[c, :]
        along = jnp.sum(that * dzt, axis=-1, keepdims=True)
        du_ref[c, :] = ((dzt - that * along) * back_ref[c, :]).astype(bf16)
    for t in tiles(du_ref.shape[1], 384):
        head_ref[t, :] = tn(du_ref[:, t], txt_ref[...]).astype(bf16)


def head_kernel(du_ref, txt_ref, got_ref, out_ref):
    for t in tiles(du_ref.shape[1], 384):
        mine = tn(du_ref[:, t], txt_ref[...])
        out_ref[t, :] = (mine + got_ref[t, :].astype(f32)).astype(bf16)


def txt_grad_kernel(tile, du_ref, head_ref, out_ref):
    for t in tiles(du_ref.shape[0], tile):
        out_ref[t, :] = nt(du_ref[t, :], head_ref[...]).astype(bf16)


def gather_kernel(pad, fold, got_ref, out_ref):
    total = got_ref[0].astype(f32)
    for k in range(1, got_ref.shape[0]):
        total = total + got_ref[k].astype(f32)
    high = total.shape[0] // fold
    for i in range(out_ref.shape[0]):
        cut = [total[high * k : high * (k + 1), pad * i : pad * (i + 1)] for k in range(fold)]
        rest = out_ref.shape[2] - fold * pad
        cut.append(jnp.zeros((high, rest), f32))
        out_ref[i] = jnp.concatenate(cut, axis=1).astype(bf16)


def image_main_kernel(tile, zi_ref, zt_ref, low_ref, high_ref, down_ref, dzi_ref, two_ref):
    two_ref[: low_ref.shape[0], :] = low_ref[...]
    two_ref[low_ref.shape[0] :, :] = high_ref[...]
    for t in tiles(zi_ref.shape[0], tile):
        zi = zi_ref[t, :]
        products = nt(zi, zt_ref[...])
        index = lax.broadcasted_iota(jnp.int32, products.shape, 1)
        total = nn(paired(products, down_ref[t, :] == index), zt_ref[...])
        dzi_ref[t, :] = total + nn(unpaired(nt(zi, two_ref[...])), two_ref[...])


def column_kernel(across_ref, out_ref):
    wide = jnp.broadcast_to(across_ref[...].astype(f32), (128, across_ref.shape[1]))
    out_ref[...] = wide.T[:, :1].astype(jnp.int32)


def image_end_kernel(tile, low_ref, high_ref, zi_ref, dzi_ref, img_ref, out_ref, zt, last):
    zt[: low_ref.shape[0], :] = low_ref[...]
    zt[low_ref.shape[0] :, :] = high_ref[...]
    for t in tiles(zi_ref.shape[0], tile):
        dsc = unpaired(nt(zi_ref[t, :], zt[...]))
        last[t, :] = nn(dsc, zt[...])
    for c in tiles(zi_ref.shape[0], 32):
        dzi = dzi_ref[c, :] + last[c, :]
        ihat, back = unit(img_ref[c, :])
        along = jnp.sum(ihat * dzi, axis=-1, keepdims=True)
        out_ref[c, :] = ((dzi - ihat * along) * back).astype(bf16)


def finish_kernel(pad, fold, devices, got_ref, out_ref):
    total = got_ref[0].astype(f32)
    for k in range(1, got_ref.shape[0]):
        total = total + got_ref[k].astype(f32)
    turned = (total * (1.0 / devices)).T
    rows = out_ref.shape[0]
    out_ref[...] = jnp.concatenate([turned[pad * k : pad * k + rows] for k in range(fold)], axis=1)


def call(kernel, outs, args, scratch=(), aliases=None, name=None, flops=1):
    return pl.pallas_call(
        kernel,
        out_shape=outs,
        scratch_shapes=list(scratch),
        input_output_aliases=aliases or {},
        compiler_params=pltpu.CompilerParams(vmem_limit_bytes=20 * MIB),
        cost_estimate=pl.CostEstimate(flops=flops, bytes_accessed=1, transcendentals=0),
        name=name,
    )(*args)


def shards(img_emb, txt_feat, head_weight, positive):
    rows, width = img_emb.shape
    n_row = lax.axis_size("row")
    n_col = lax.axis_size("col")
    share_rows = width // n_row
    share_cols = width // n_col
    depth = n_row // 4
    tile = rows
    shape = jax.ShapeDtypeStruct

    def after(value, *others):
        return lax.optimization_barrier((value,) + others)[0]

    half = rows // 2
    img_one = from_partner(img_emb, "row", n_row // 2)
    img_two = from_partner(img_emb, "col", n_col // 2)

    core = lax.axis_index("row") & 1
    pad = -(-share_rows // 8) * 8
    lanes = 2 * depth * pad
    lane = jnp.arange(lanes, dtype=jnp.int32)
    place = lane // pad
    inner = lane % pad
    block = (place % depth) * 4 + (place // depth) * 2

    def sources(which):
        return jnp.where(inner < share_rows, (block + which) * share_rows + inner, -1)[None, :]

    step = rows // 2
    that, tback, zt, zt_low, zt_high, txt_mine, txt_theirs = pl.pallas_call(
        text_kernel,
        grid=(2,),
        in_specs=[
            pl.BlockSpec((step, width), lambda i: (i, 0)),
            pl.BlockSpec((width, width), lambda i: (0, 0)),
            pl.BlockSpec((1, lanes), lambda i: (0, 0)),
            pl.BlockSpec((1, lanes), lambda i: (0, 0)),
        ],
        out_specs=[
            pl.BlockSpec((step, width), lambda i: (i, 0)),
            pl.BlockSpec((step, 1), lambda i: (i, 0)),
            pl.BlockSpec((step, width), lambda i: (i, 0)),
            pl.BlockSpec((step, width), lambda i: (0, 0)),
            pl.BlockSpec((step, width), lambda i: (0, 0)),
            pl.BlockSpec((step, lanes), lambda i: (i, 0)),
            pl.BlockSpec((step, lanes), lambda i: (i, 0)),
        ],
        out_shape=[
            shape((rows, width), f32),
            shape((rows, 1), f32),
            shape((rows, width), bf16),
            shape((step, width), bf16),
            shape((step, width), bf16),
            shape((rows, lanes), bf16),
            shape((rows, lanes), bf16),
        ],
        scratch_shapes=[pltpu.VMEM((2, width, lanes), bf16)],
        compiler_params=pltpu.CompilerParams(vmem_limit_bytes=16 * MIB),
        cost_estimate=pl.CostEstimate(flops=1, bytes_accessed=1, transcendentals=0),
        name="text",
    )(txt_feat, head_weight, sources(core), sources(1 - core))
    txt_two = [from_partner(part, "col", n_col // 2) for part in (zt_low, zt_high)]

    wide = shape((rows, width), f32)
    narrow = shape((rows, width), bf16)
    zi, dzt = call(
        functools.partial(text_main_kernel, tile),
        [narrow, wide],
        [img_emb, img_two, zt, positive],
        [pltpu.VMEM((rows, width), bf16)],
        name="text_main",
    )
    du, head = call(
        functools.partial(text_end_kernel, tile, 1),
        [narrow, shape((width, lanes), bf16)],
        [img_one, zt, after(dzt, *txt_two), that, tback, txt_theirs],
        [pltpu.VMEM((rows, width), bf16), pltpu.VMEM((rows, width), f32)],
        name="text_end",
    )
    head = from_partner(head, "row", 1)
    head = call(
        head_kernel,
        shape((width, lanes), bf16),
        [du, txt_mine, head],
        name="head",
    )
    txt_a = turn(after(zt_low, du), 1)
    txt_b = turn(after(zt_high, du), -1)
    du_late = after(du, head)
    head = lax.all_to_all(head.reshape(n_col, share_cols, lanes), "col", 0, 0, tiled=True)
    txt_grad = call(
        functools.partial(txt_grad_kernel, tile), narrow, [du_late, head_weight], name="txt_grad"
    )
    down = call(
        column_kernel,
        shape((rows, 1), jnp.int32),
        [after(positive, txt_a, txt_b, txt_grad)],
        name="column",
        flops=int(X_FIRST),
    )
    txt_a = turn(after(txt_a, down), depth // 2 - 2)
    txt_b = turn(after(txt_b, down), 2 - depth // 2)
    dzi = call(
        functools.partial(image_main_kernel, tile),
        wide,
        [zi, zt, *txt_two, down],
        [pltpu.VMEM((rows, width), bf16)],
        name="image_main",
    )
    head = after(head, dzi, txt_grad)
    fold = 3
    head = call(
        functools.partial(gather_kernel, pad, fold),
        shape((2 * depth, share_cols // fold, 128), bf16),
        [head],
        name="gather",
    )
    groups = [[z * 4 + y * 2 + c for y in range(2) for z in range(depth)] for c in range(2)]
    head = lax.all_to_all(head, "row", 0, 0, axis_index_groups=groups, tiled=True)
    txt_a = turn(after(txt_a, dzi), 1)
    txt_b = turn(after(txt_b, dzi), -1)
    head_grad = call(
        functools.partial(finish_kernel, pad, fold, n_row * n_col),
        shape((share_rows, share_cols), f32),
        [head],
        name="finish",
        flops=int(X_FINISH),
    )
    img_grad = call(
        functools.partial(image_end_kernel, tile),
        narrow,
        [txt_a, txt_b, zi, after(dzi, head_grad), img_emb],
        [pltpu.VMEM((rows, width), bf16), pltpu.VMEM((rows, width), f32)],
        name="image_end",
        flops=int(X_END),
    )
    return (img_grad, txt_grad, head_grad)


def solution(mesh):
    return jax.shard_map(
        shards,
        mesh=mesh,
        in_specs=(P(("row", "col"), None), P(("row", "col"), None), P(), P(("row", "col"), None)),
        out_specs=(P(("row", "col"), None), P(("row", "col"), None), P("row", "col")),
        check_vma=False,
    )
```

```python
import functools

import jax
import jax.numpy as jnp
from jax import lax
from jax.experimental import pallas as pl
from jax.experimental.pallas import tpu as pltpu
from jax.sharding import PartitionSpec as P

scale_logit = 8.0
bias_logit = -2.0
f32 = jnp.float32
bf16 = jnp.bfloat16
MIB = 1 << 20
X_FIRST = 6.5e9
X_FINISH = 6e9
X_END = 3e9


def from_partner(block, axis, mask):
    count = lax.axis_size(axis)
    return lax.ppermute(block, axis, [(low, low ^ mask) for low in range(count)])


def turn(block, by):
    count = lax.axis_size("row")
    return lax.ppermute(block, "row", [(at, (at + 4 * by) % count) for at in range(count)])


def nt(a, b):
    return lax.dot_general(a, b, (((1,), (1,)), ((), ())), preferred_element_type=f32)


def tn(a, b):
    return lax.dot_general(a, b, (((0,), (0,)), ((), ())), preferred_element_type=f32)


def nn(a, b):
    return jnp.dot(a, b, preferred_element_type=f32)


def unit(block):
    wide = block.astype(f32)
    back = 1.0 / jnp.sqrt(jnp.sum(wide * wide, axis=-1, keepdims=True) + 1e-06)
    return wide * back, back


def unpaired(products):
    return (scale_logit / (1.0 + jnp.exp(-bias_logit - scale_logit * products))).astype(bf16)


def paired(products, labels):
    logits = scale_logit * products + bias_logit
    size = scale_logit / (1.0 + jnp.exp(jnp.where(labels, logits, -logits)))
    return jnp.where(labels, -size, size).astype(bf16)


def tiles(rows, size):
    return [slice(at, at + size) for at in range(0, rows, size)]


def text_kernel(txt_ref, head_ref, mine_ref, theirs_ref, that_ref, back_ref, zt_ref, low_ref, high_ref, my_ref, their_ref, choose):
    width = head_ref.shape[0]

    @pl.when(pl.program_id(0) == 0)
    def _():
        for k, source_ref in enumerate((mine_ref, theirs_ref)):
            index = lax.broadcasted_iota(jnp.int32, (width, source_ref.shape[1]), 0)
            choose[k] = jnp.where(source_ref[...] == index, 1.0, 0.0).astype(bf16)

    txt = txt_ref[...]
    u = nn(txt, head_ref[...])
    back = 1.0 / jnp.sqrt(jnp.sum(u * u, axis=-1, keepdims=True) + 1e-06)
    that = u * back
    that_ref[...] = that
    back_ref[...] = back
    zt_ref[...] = that.astype(bf16)

    @pl.when(pl.program_id(0) == 0)
    def _():
        low_ref[...] = that.astype(bf16)

    @pl.when(pl.program_id(0) == 1)
    def _():
        high_ref[...] = that.astype(bf16)

    my_ref[...] = nn(txt, choose[0]).astype(bf16)
    their_ref[...] = nn(txt, choose[1]).astype(bf16)


def load_units(pieces, zi):
    at = 0
    for piece in pieces:
        for c in tiles(piece.shape[0], 32):
            zi[at + c.start : at + c.stop, :] = unit(piece[c, :])[0].astype(bf16)
        at += piece.shape[0]


def text_main_kernel(tile, img_ref, two_ref, zt_ref, across_ref, zi_ref, dzt_ref, zi):
    load_units([img_ref], zi_ref)
    load_units([two_ref], zi)
    for t in tiles(zt_ref.shape[0], tile):
        zt = zt_ref[t, :]
        products = nt(zt, zi_ref[...])
        index = lax.broadcasted_iota(jnp.int32, products.shape, 0) + t.start
        total = nn(paired(products, across_ref[...] == index), zi_ref[...])
        dzt_ref[t, :] = total + nn(unpaired(nt(zt, zi[...])), zi[...])


def text_end_kernel(tile, count, *refs):
    pieces = refs[:count]
    zt_ref, dzt_ref, that_ref, back_ref, txt_ref, du_ref, head_ref, zi, last = refs[count:]
    load_units(pieces, zi)
    for t in tiles(zt_ref.shape[0], tile):
        dsc = unpaired(nt(zt_ref[t, :], zi[...]))
        last[t, :] = nn(dsc, zi[...])
    for c in tiles(zt_ref.shape[0], 32):
        dzt = dzt_ref[c, :] + last[c, :]
        that = that_ref[c, :]
        along = jnp.sum(that * dzt, axis=-1, keepdims=True)
        du_ref[c, :] = ((dzt - that * along) * back_ref[c, :]).astype(bf16)
    for t in tiles(du_ref.shape[1], 384):
        head_ref[t, :] = tn(du_ref[:, t], txt_ref[...]).astype(bf16)


def head_kernel(du_ref, txt_ref, got_ref, out_ref):
    for t in tiles(du_ref.shape[1], 384):
        mine = tn(du_ref[:, t], txt_ref[...])
        out_ref[t, :] = (mine + got_ref[t, :].astype(f32)).astype(bf16)


def txt_grad_kernel(tile, du_ref, head_ref, out_ref):
    for t in tiles(du_ref.shape[0], tile):
        out_ref[t, :] = nt(du_ref[t, :], head_ref[...]).astype(bf16)


def gather_kernel(pad, fold, got_ref, out_ref):
    total = got_ref[0].astype(f32)
    for k in range(1, got_ref.shape[0]):
        total = total + got_ref[k].astype(f32)
    high = total.shape[0] // fold
    for i in range(out_ref.shape[0]):
        cut = [total[high * k : high * (k + 1), pad * i : pad * (i + 1)] for k in range(fold)]
        rest = out_ref.shape[2] - fold * pad
        cut.append(jnp.zeros((high, rest), f32))
        out_ref[i] = jnp.concatenate(cut, axis=1).astype(bf16)


def image_main_kernel(tile, zi_ref, zt_ref, low_ref, high_ref, down_ref, dzi_ref, two_ref):
    two_ref[: low_ref.shape[0], :] = low_ref[...]
    two_ref[low_ref.shape[0] :, :] = high_ref[...]
    for t in tiles(zi_ref.shape[0], tile):
        zi = zi_ref[t, :]
        products = nt(zi, zt_ref[...])
        index = lax.broadcasted_iota(jnp.int32, products.shape, 1)
        total = nn(paired(products, down_ref[t, :] == index), zt_ref[...])
        dzi_ref[t, :] = total + nn(unpaired(nt(zi, two_ref[...])), two_ref[...])


def column_kernel(across_ref, out_ref):
    wide = jnp.broadcast_to(across_ref[...].astype(f32), (128, across_ref.shape[1]))
    out_ref[...] = wide.T[:, :1].astype(jnp.int32)


def image_end_kernel(tile, low_ref, high_ref, zi_ref, dzi_ref, img_ref, out_ref, zt, last):
    zt[: low_ref.shape[0], :] = low_ref[...]
    zt[low_ref.shape[0] :, :] = high_ref[...]
    for t in tiles(zi_ref.shape[0], tile):
        dsc = unpaired(nt(zi_ref[t, :], zt[...]))
        last[t, :] = nn(dsc, zt[...])
    for c in tiles(zi_ref.shape[0], 32):
        dzi = dzi_ref[c, :] + last[c, :]
        img = img_ref[c, :].astype(f32)
        square = jnp.sum(img * img, axis=-1, keepdims=True) + 1e-06
        along = jnp.sum(img * dzi, axis=-1, keepdims=True) / square
        out_ref[c, :] = ((dzi - img * along) * (1.0 / jnp.sqrt(square))).astype(bf16)


def finish_kernel(pad, fold, devices, got_ref, out_ref):
    total = got_ref[0].astype(f32)
    for k in range(1, got_ref.shape[0]):
        total = total + got_ref[k].astype(f32)
    turned = (total * (1.0 / devices)).T
    rows = out_ref.shape[0]
    out_ref[...] = jnp.concatenate([turned[pad * k : pad * k + rows] for k in range(fold)], axis=1)


def call(kernel, outs, args, scratch=(), aliases=None, name=None, flops=1):
    return pl.pallas_call(
        kernel,
        out_shape=outs,
        scratch_shapes=list(scratch),
        input_output_aliases=aliases or {},
        compiler_params=pltpu.CompilerParams(vmem_limit_bytes=20 * MIB),
        cost_estimate=pl.CostEstimate(flops=flops, bytes_accessed=1, transcendentals=0),
        name=name,
    )(*args)


def shards(img_emb, txt_feat, head_weight, positive):
    rows, width = img_emb.shape
    n_row = lax.axis_size("row")
    n_col = lax.axis_size("col")
    share_rows = width // n_row
    share_cols = width // n_col
    depth = n_row // 4
    tile = rows
    shape = jax.ShapeDtypeStruct

    def after(value, *others):
        return lax.optimization_barrier((value,) + others)[0]

    half = rows // 2
    img_one = from_partner(img_emb, "row", n_row // 2)
    img_two = from_partner(img_emb, "col", n_col // 2)

    core = lax.axis_index("row") & 1
    pad = -(-share_rows // 8) * 8
    lanes = 2 * depth * pad
    lane = jnp.arange(lanes, dtype=jnp.int32)
    place = lane // pad
    inner = lane % pad
    block = (place % depth) * 4 + (place // depth) * 2

    def sources(which):
        return jnp.where(inner < share_rows, (block + which) * share_rows + inner, -1)[None, :]

    step = rows // 2
    that, tback, zt, zt_low, zt_high, txt_mine, txt_theirs = pl.pallas_call(
        text_kernel,
        grid=(2,),
        in_specs=[
            pl.BlockSpec((step, width), lambda i: (i, 0)),
            pl.BlockSpec((width, width), lambda i: (0, 0)),
            pl.BlockSpec((1, lanes), lambda i: (0, 0)),
            pl.BlockSpec((1, lanes), lambda i: (0, 0)),
        ],
        out_specs=[
            pl.BlockSpec((step, width), lambda i: (i, 0)),
            pl.BlockSpec((step, 1), lambda i: (i, 0)),
            pl.BlockSpec((step, width), lambda i: (i, 0)),
            pl.BlockSpec((step, width), lambda i: (0, 0)),
            pl.BlockSpec((step, width), lambda i: (0, 0)),
            pl.BlockSpec((step, lanes), lambda i: (i, 0)),
            pl.BlockSpec((step, lanes), lambda i: (i, 0)),
        ],
        out_shape=[
            shape((rows, width), f32),
            shape((rows, 1), f32),
            shape((rows, width), bf16),
            shape((step, width), bf16),
            shape((step, width), bf16),
            shape((rows, lanes), bf16),
            shape((rows, lanes), bf16),
        ],
        scratch_shapes=[pltpu.VMEM((2, width, lanes), bf16)],
        compiler_params=pltpu.CompilerParams(vmem_limit_bytes=16 * MIB),
        cost_estimate=pl.CostEstimate(flops=1, bytes_accessed=1, transcendentals=0),
        name="text",
    )(txt_feat, head_weight, sources(core), sources(1 - core))
    txt_two = [from_partner(part, "col", n_col // 2) for part in (zt_low, zt_high)]

    wide = shape((rows, width), f32)
    narrow = shape((rows, width), bf16)
    zi, dzt = call(
        functools.partial(text_main_kernel, tile),
        [narrow, wide],
        [img_emb, img_two, zt, positive],
        [pltpu.VMEM((rows, width), bf16)],
        name="text_main",
    )
    du, head = call(
        functools.partial(text_end_kernel, tile, 1),
        [narrow, shape((width, lanes), bf16)],
        [img_one, zt, after(dzt, *txt_two), that, tback, txt_theirs],
        [pltpu.VMEM((rows, width), bf16), pltpu.VMEM((rows, width), f32)],
        name="text_end",
    )
    head = from_partner(head, "row", 1)
    head = call(
        head_kernel,
        shape((width, lanes), bf16),
        [du, txt_mine, head],
        name="head",
    )
    txt_a = turn(after(zt_low, du), 1)
    txt_b = turn(after(zt_high, du), -1)
    du_late = after(du, head)
    head = lax.all_to_all(head.reshape(n_col, share_cols, lanes), "col", 0, 0, tiled=True)
    txt_grad = call(
        functools.partial(txt_grad_kernel, tile), narrow, [du_late, head_weight], name="txt_grad"
    )
    down = call(
        column_kernel,
        shape((rows, 1), jnp.int32),
        [after(positive, txt_a, txt_b, txt_grad)],
        name="column",
        flops=int(X_FIRST),
    )
    txt_a = turn(after(txt_a, down), depth // 2 - 2)
    txt_b = turn(after(txt_b, down), 2 - depth // 2)
    dzi = call(
        functools.partial(image_main_kernel, tile),
        wide,
        [zi, zt, *txt_two, down],
        [pltpu.VMEM((rows, width), bf16)],
        name="image_main",
    )
    head = after(head, dzi, txt_grad)
    fold = 3
    head = call(
        functools.partial(gather_kernel, pad, fold),
        shape((2 * depth, share_cols // fold, 128), bf16),
        [head],
        name="gather",
    )
    groups = [[z * 4 + y * 2 + c for y in range(2) for z in range(depth)] for c in range(2)]
    head = lax.all_to_all(head, "row", 0, 0, axis_index_groups=groups, tiled=True)
    txt_a = turn(after(txt_a, dzi), 1)
    txt_b = turn(after(txt_b, dzi), -1)
    head_grad = call(
        functools.partial(finish_kernel, pad, fold, n_row * n_col),
        shape((share_rows, share_cols), f32),
        [head],
        name="finish",
        flops=int(X_FINISH),
    )
    img_grad = call(
        functools.partial(image_end_kernel, tile),
        narrow,
        [txt_a, txt_b, zi, after(dzi, head_grad), img_emb],
        [pltpu.VMEM((rows, width), bf16), pltpu.VMEM((rows, width), f32)],
        name="image_end",
        flops=int(X_END),
    )
    return (img_grad, txt_grad, head_grad)


def solution(mesh):
    return jax.shard_map(
        shards,
        mesh=mesh,
        in_specs=(P(("row", "col"), None), P(("row", "col"), None), P(), P(("row", "col"), None)),
        out_specs=(P(("row", "col"), None), P(("row", "col"), None), P("row", "col")),
        check_vma=False,
    )
```
